32 devices in a mesh: slab: 4 (over y, core), hst: 8 (over z, x).
Axes of the slice: x: 2, y: 2, z: 4, core: 2. Of those that a mesh axis runs over, the one named last changes fastest.
Arguments:
- load: bfloat16 [288, 65536], P('slab', 'hst'), may hold values from -6 to 6
- host_rack: int32 [65536], P('hst'), may hold values from 0 to 2047, as said below
- rack_pod: int32 [2048], P('hst'), may hold values from 0 to 15
Outputs:
- host_drift: float32 [288, 65536], P('slab', 'hst')
- rack_drift: float32 [288, 2048], P('slab', 'hst')
- pod_drift: float32 [288, 16], P('slab', 'hst')
The draws below stay inside these ranges and needn't reach their ends.
Inputs may be any that keep to these rules, and one draw needn't show every extreme that they name: `host_rack`: the hosts s * 8192 to (s + 1) * 8192 - 1 belong to racks among s * 256 to (s + 2) * 256 - 1, counted modulo 2048; racks hold uneven numbers of hosts, some none.
All inputs are finite; a program needn't handle non-finite values.
Results may differ from the reference program's by a relative error of at most 0.0003.
Values may be sent and summed in bfloat16 or wider, within the bound.
A program may use at most 64 MiB of HBM per device.

```python
import math
import jax
import jax.numpy as jnp

SLAB_LEN = 36
STEPS = 288
H_DEV = 8192
R_DEV = 256
POD_DEV = 2
HOSTS = 65536
RACKS = 2048
PODS = 16


def draw_host_rack(key, part):
    shard_count = HOSTS // H_DEV
    key_rate = jax.random.fold_in(key, 11)
    key_dice = jax.random.fold_in(key, 12)
    key_first = jax.random.fold_in(key, 13)
    key_second = jax.random.fold_in(key, 14)
    host_ids = jnp.arange(HOSTS, dtype=jnp.int32)
    shard_of = host_ids // H_DEV
    local_index = host_ids % H_DEV
    spill_rate = jax.random.randint(key_rate, (shard_count,), 10, 91)
    dice_roll = jax.random.randint(key_dice, (HOSTS,), 0, 100)
    spilled = (dice_roll < spill_rate[shard_of]).astype(jnp.int32)
    first_pick = jax.random.randint(key_first, (HOSTS,), 0, R_DEV)
    second_pick = jax.random.randint(key_second, (HOSTS,), 0, R_DEV)
    within_shard = jnp.where(spilled == 1, first_pick, jnp.minimum(first_pick, second_pick))
    within_shard = jnp.where(local_index == H_DEV - 1, R_DEV - 1, within_shard)
    within_shard = jnp.where(local_index == 0, 0, within_shard)
    spilled = jnp.where((local_index == 0) | (local_index == H_DEV - 1), 0, spilled)
    return (((shard_of + spilled) * R_DEV + within_shard) % RACKS).astype(jnp.int32)


def set_ends(array, key, smallest, top_value):
    longest = array.shape.index(max(array.shape))
    spots = []
    for shift in (0, 1):
        where = [jax.random.randint(jax.random.fold_in(key, axis), (), 0, length) for axis, length in enumerate(array.shape)]
        where[longest] = (where[longest] + shift) % array.shape[longest]
        spots.append(tuple(where))
    return array.at[spots[0]].set(smallest).at[spots[1]].set(top_value)


def shard_levels(own_key, dims, pieces, low, top_value):
    level = 1.0
    for dim, parts in pieces:
        draws = jax.random.uniform(jax.random.fold_in(jax.random.fold_in(own_key, 6), dim), (parts,), jnp.float32, low / len(pieces), top_value / len(pieces))
        level = level * jnp.repeat(jnp.exp(draws), dims[dim] // parts).reshape((-1,) + (1,) * (len(dims) - 1 - dim))
    return level


def normal_values(key, shape, width, most, pieces=(), kind=jnp.bfloat16):
    gain = shard_levels(key, shape, pieces, -0.22, 0.18) if pieces else 1.0
    result = jax.random.normal(key, shape, jnp.float32) * width * gain
    return jnp.minimum(jnp.maximum(result, -most), most).astype(kind)


def setup_inputs(seed: int = 0) -> dict:
    streams_of = jax.random.split(jax.random.key(seed), 4)
    load = normal_values(streams_of[0], (STEPS, HOSTS), 1.0, 6.0, ((0, 4), (1, 8)))
    host_rack = draw_host_rack(jax.random.fold_in(streams_of[3], 71), 0)
    rack_pod = set_ends(jax.random.randint(streams_of[2], (RACKS,), 0, PODS), jax.random.fold_in(streams_of[2], 1), 0, PODS - 1).astype(jnp.int32)
    return {"load": load, "host_rack": host_rack, "rack_pod": rack_pod}


def windowed(series, half_window):
    total_steps = series.shape[0]
    extended = jnp.concatenate([series[total_steps - half_window:], series, series[:half_window]], 0)
    zero_row = jnp.zeros((1, series.shape[1]), jnp.float32)
    running = jnp.concatenate([zero_row, jnp.cumsum(extended, axis=0)], 0)
    return running[2 * half_window + 1:] - running[:total_steps]

def reference(load, host_rack, rack_pod):
    half_window = 2 * SLAB_LEN
    window_size = 2 * half_window + 1
    series = load.astype(jnp.float32)
    baseline = windowed(series, half_window) / window_size
    deviation = series - baseline
    host_sum = jnp.cumsum(deviation, axis=0)
    rack_sum = jax.ops.segment_sum(host_sum.T, host_rack, num_segments=RACKS).T
    pod_sum = jax.ops.segment_sum(rack_sum.T, rack_pod, num_segments=PODS).T
    host_drift = host_sum * (1.0 / math.sqrt(STEPS))
    rack_drift = rack_sum * (1.0 / math.sqrt(STEPS * H_DEV / R_DEV))
    pod_drift = pod_sum * (1.0 / math.sqrt(STEPS * H_DEV / POD_DEV))
    return (host_drift, rack_drift, pod_drift)
```

```python
import functools
import math

import jax
import jax.numpy as jnp
from jax import lax
from jax.experimental import pallas as pl
from jax.experimental.pallas import tpu as pltpu
from jax.sharding import PartitionSpec as P

SLAB_LEN = 36
POD_DEV = 2
SLABS = 4
PARTS = 8
MESH = pl.DeviceIdType.MESH
EXACT = lax.Precision.HIGHEST
NT = (((1,), (1,)), ((), ()))


def coefficients(target, source, out_rows, rows):
    reach = 2 * SLAB_LEN
    day = SLABS * rows
    t = target * rows + lax.broadcasted_iota(jnp.int32, (out_rows, rows), 0)
    u = source * rows + lax.broadcasted_iota(jnp.int32, (out_rows, rows), 1)
    value = jnp.where(u <= t, 2 * reach + 1, 0)
    for wrap in (-day, 0, day):
        first = jnp.maximum(u + (wrap - reach), 0)
        last = jnp.minimum(u + (wrap + reach), t)
        value = value - jnp.maximum(last - first + 1, 0)
    return value.astype(jnp.float32)


def kernel(
    shards,
    load_hbm,
    rack_ref,
    pod_ref,
    host_out,
    rack_out,
    pod_out,
    own,
    near,
    far,
    local_rack,
    partial,
    spill,
    totals,
    near_totals,
    far_totals,
    pod_terms,
    pod_in,
    pod_sum,
    slab_pods,
    rack_row,
    rack_row_in,
    host_row,
    host_row_in,
    load_sem,
    near_sems,
    far_send,
    far_recv,
    small_send,
    small_recv,
    pod_send,
    pod_recv,
):
    rows, hosts = own.shape
    racks = totals.shape[1]
    width = hosts // PARTS
    d = lax.axis_index("slab")
    h = lax.axis_index("hst")
    odd = lax.rem(d, 2)
    near_d = d + 1 - 2 * odd
    far_d = lax.rem(d + 3 + 2 * odd, SLABS)
    diag_d = lax.rem(d + 2, SLABS)
    window = 4 * SLAB_LEN + 1
    day = SLABS * rows

    barrier = pltpu.get_barrier_semaphore()
    for peer in (near_d, far_d, diag_d):
        pl.semaphore_signal(barrier, inc=1, device_id=(peer, h), device_id_type=MESH)

    @pl.loop(1, shards)
    def _(k):
        peer = lax.rem(h + k, shards)
        pl.semaphore_signal(barrier, inc=1, device_id=(d, peer), device_id_type=MESH)

    load_copy = pltpu.make_async_copy(load_hbm, own, load_sem)
    load_copy.start()
    local = rack_ref[...] - h * racks
    local_rack[...] = jnp.where(local < 0, local + racks * shards, local)
    pl.semaphore_wait(barrier, SLABS - 1 + shards - 1)

    def far_copy(c):
        cols = pl.ds(pl.multiple_of(c * width, width), width)
        return pltpu.make_async_remote_copy(
            src_ref=load_hbm.at[:, cols],
            dst_ref=far.at[:, cols],
            send_sem=far_send.at[c],
            recv_sem=far_recv.at[c],
            device_id=(far_d, h),
            device_id_type=MESH,
        )

    def small_copy(src, dst, index, device):
        return pltpu.make_async_remote_copy(
            src_ref=src,
            dst_ref=dst,
            send_sem=small_send.at[index],
            recv_sem=small_recv.at[index],
            device_id=device,
            device_id_type=MESH,
        )

    for c in range(PARTS):
        far_copy(c).start()
    near_copy = pltpu.make_async_remote_copy(
        src_ref=load_hbm,
        dst_ref=near,
        send_sem=near_sems.at[0],
        recv_sem=near_sems.at[1],
        device_id=(near_d, h),
        device_id_type=MESH,
    )
    near_copy.start()
    load_copy.wait()

    partial[...] = jnp.zeros_like(partial)
    rack_ids = lax.broadcasted_iota(jnp.int32, (2 * racks, 128), 0)

    @pl.loop(0, PARTS)
    def _(c):
        cols = pl.ds(pl.multiple_of(c * width, width), width)
        member = jnp.concatenate(
            [
                (rack_ids == local_rack[pl.ds(c * (width // 128) + k, 1), :])
                .astype(jnp.float32)
                .astype(jnp.bfloat16)
                for k in range(width // 128)
            ],
            axis=1,
        )
        partial[...] += lax.dot_general(
            own[:, cols], member, NT, preferred_element_type=jnp.float32
        )

    spill_copy = small_copy(
        partial.at[:, pl.ds(racks, racks)], spill, 0, (d, lax.rem(h + 1, shards))
    )
    spill_copy.start()

    k_own = coefficients(d, d, rows, rows)
    k_near = coefficients(d, near_d, rows, rows)
    k_far = coefficients(d, far_d, rows, rows)
    k_diag = coefficients(diag_d, d, 8, rows)
    k_both = jnp.concatenate([k_own, k_diag], 0).astype(jnp.bfloat16)

    @pl.loop(0, PARTS)
    def _(c):
        cols = pl.ds(pl.multiple_of(c * width, width), width)
        both = jnp.dot(k_both, own[:, cols], preferred_element_type=jnp.float32)
        host_out[:, cols] = both[:rows]
        host_row[pl.ds(c, 1), :] = both[rows : rows + 1]

    host_row_copy = small_copy(host_row, host_row_in, 1, (diag_d, h))
    host_row_copy.start()

    spill_copy.wait()
    totals[...] = partial[:, :racks] + spill[...]
    slots = lax.broadcasted_iota(jnp.int32, (8 * shards, 128), 0)
    slot_pod = jnp.where(slots % 8 < POD_DEV, slots // 8 * POD_DEV + slots % 8, -1)
    pod_member = jnp.concatenate(
        [
            (slot_pod == pod_ref[pl.ds(k, 1), :]).astype(jnp.float32)
            for k in range(racks // 128)
        ],
        axis=1,
    )
    pod_terms[...] = lax.dot_general(
        pod_member, totals[...], NT, preferred_element_type=jnp.float32, precision=EXACT
    )

    def pod_copy(k):
        peer = lax.rem(h + k, shards)
        return pltpu.make_async_remote_copy(
            src_ref=pod_terms.at[pl.ds(pl.multiple_of(peer * 8, 8), 8), :],
            dst_ref=pod_in.at[k],
            send_sem=pod_send.at[k],
            recv_sem=pod_recv.at[k],
            device_id=(d, peer),
            device_id_type=MESH,
        )

    @pl.loop(1, shards)
    def _(k):
        pod_copy(k).start()

    rack_row[...] = jnp.dot(
        k_diag, totals[...], preferred_element_type=jnp.float32, precision=EXACT
    )
    copies = [
        small_copy(totals, far_totals, 2, (far_d, h)),
        small_copy(rack_row, rack_row_in, 3, (diag_d, h)),
        small_copy(totals, near_totals, 4, (near_d, h)),
    ]
    for copy in copies:
        copy.start()

    near_copy.wait()
    k_near_half = k_near.astype(jnp.bfloat16)

    @pl.loop(0, PARTS)
    def _(c):
        cols = pl.ds(pl.multiple_of(c * width, width), width)
        host_out[:, cols] += jnp.dot(
            k_near_half, near[:, cols], preferred_element_type=jnp.float32
        )

    pod_sum[...] = pod_terms[pl.ds(pl.multiple_of(h * 8, 8), 8), :]

    @pl.loop(1, shards)
    def _(k):
        pod_copy(k).wait()
        pod_sum[...] += pod_in[k]

    pod_copies = [
        small_copy(pod_sum, slab_pods.at[0], 5, (far_d, h)),
        small_copy(pod_sum, slab_pods.at[1], 6, (diag_d, h)),
        small_copy(pod_sum, slab_pods.at[2], 7, (near_d, h)),
    ]
    for copy in pod_copies:
        copy.start()

    host_row_copy.wait()
    k_far_half = k_far.astype(jnp.bfloat16)
    host_scale = 1.0 / (window * math.sqrt(day))

    def finish(c):
        cols = pl.ds(pl.multiple_of(c * width, width), width)
        far_copy(c).wait()
        host_out[:, cols] = (
            host_out[:, cols]
            + jnp.dot(k_far_half, far[:, cols], preferred_element_type=jnp.float32)
            + host_row_in[pl.ds(c, 1), :]
        ) * host_scale

    @pl.loop(0, PARTS - 2)
    def _(c):
        finish(c)

    for copy in copies + pod_copies:
        copy.wait()

    def exact(a, b):
        return jnp.dot(a, b, preferred_element_type=jnp.float32, precision=EXACT)

    def exact_nt(a, b):
        return lax.dot_general(a, b, NT, preferred_element_type=jnp.float32, precision=EXACT)

    rack_scale = 1.0 / (window * math.sqrt(day * hosts / racks))
    rack_out[...] = (
        exact(k_own, totals[...])
        + exact(k_near, near_totals[...])
        + exact(k_far, far_totals[...])
        + rack_row_in[0:1, :]
    ) * rack_scale
    pod_scale = 1.0 / (window * math.sqrt(day * hosts / POD_DEV))
    pods = (
        exact_nt(pod_sum[...], k_own)
        + exact_nt(slab_pods[0], k_far)
        + exact_nt(slab_pods[1], coefficients(d, diag_d, rows, rows))
        + exact_nt(slab_pods[2], k_near)
    ) * pod_scale
    pod_out[...] = pods[:POD_DEV]

    @pl.loop(PARTS - 2, PARTS)
    def _(c):
        finish(c)


def on_device(load, host_rack, rack_pod):
    rows, hosts = load.shape
    racks = rack_pod.shape[0]
    shards = lax.axis_size("hst")
    f32 = jnp.float32
    vmem = pl.BlockSpec(memory_space=pltpu.VMEM)
    host, rack, pod = pl.pallas_call(
        functools.partial(kernel, shards),
        out_shape=(
            jax.ShapeDtypeStruct((rows, hosts), f32),
            jax.ShapeDtypeStruct((rows, racks), f32),
            jax.ShapeDtypeStruct((POD_DEV, rows), f32),
        ),
        in_specs=[pl.BlockSpec(memory_space=pl.ANY), vmem, vmem],
        out_specs=(vmem, vmem, vmem),
        scratch_shapes=[
            pltpu.VMEM((rows, hosts), load.dtype),
            pltpu.VMEM((rows, hosts), load.dtype),
            pltpu.VMEM((rows, hosts), load.dtype),
            pltpu.VMEM((hosts // 128, 128), jnp.int32),
            pltpu.VMEM((rows, 2 * racks), f32),
            pltpu.VMEM((rows, racks), f32),
            pltpu.VMEM((rows, racks), f32),
            pltpu.VMEM((rows, racks), f32),
            pltpu.VMEM((rows, racks), f32),
            pltpu.VMEM((8 * shards, rows), f32),
            pltpu.VMEM((shards, 8, rows), f32),
            pltpu.VMEM((8, rows), f32),
            pltpu.VMEM((SLABS - 1, 8, rows), f32),
            pltpu.VMEM((8, racks), f32),
            pltpu.VMEM((8, racks), f32),
            pltpu.VMEM((PARTS, hosts // PARTS), f32),
            pltpu.VMEM((PARTS, hosts // PARTS), f32),
            pltpu.SemaphoreType.DMA,
            pltpu.SemaphoreType.DMA((2,)),
            pltpu.SemaphoreType.DMA((PARTS,)),
            pltpu.SemaphoreType.DMA((PARTS,)),
            pltpu.SemaphoreType.DMA((8,)),
            pltpu.SemaphoreType.DMA((8,)),
            pltpu.SemaphoreType.DMA((shards,)),
            pltpu.SemaphoreType.DMA((shards,)),
        ],
        compiler_params=pltpu.CompilerParams(
            collective_id=0, has_side_effects=True, vmem_limit_bytes=40 * 1024 * 1024
        ),
        cost_estimate=pl.CostEstimate(
            flops=2 * rows * hosts * (3 * rows + 2 * racks),
            bytes_accessed=rows * hosts * 10,
            transcendentals=0,
        ),
    )(load, host_rack.reshape(hosts // 128, 128), rack_pod.reshape(racks // 128, 128))
    return host, rack, pod.T


def solution(mesh):
    in_specs = (P("slab", "hst"), P("hst"), P("hst"))
    out_specs = (P("slab", "hst"), P("slab", "hst"), P("slab", "hst"))
    return jax.shard_map(
        on_device, mesh=mesh, in_specs=in_specs, out_specs=out_specs, check_vma=False
    )
```

```python
import functools
import math

import jax
import jax.numpy as jnp
from jax import lax
from jax.experimental import pallas as pl
from jax.experimental.pallas import tpu as pltpu
from jax.sharding import PartitionSpec as P

SLAB_LEN = 36
POD_DEV = 2
SLABS = 4
PARTS = 8
AHEAD = 3
MESH = pl.DeviceIdType.MESH
EXACT = lax.Precision.HIGHEST
NT = (((1,), (1,)), ((), ()))


def coefficients(target, source, out_rows, rows):
    reach = 2 * SLAB_LEN
    day = SLABS * rows
    t = target * rows + lax.broadcasted_iota(jnp.int32, (out_rows, rows), 0)
    u = source * rows + lax.broadcasted_iota(jnp.int32, (out_rows, rows), 1)
    value = jnp.where(u <= t, 2 * reach + 1, 0)
    for wrap in (-day, 0, day):
        first = jnp.maximum(u + (wrap - reach), 0)
        last = jnp.minimum(u + (wrap + reach), t)
        value = value - jnp.maximum(last - first + 1, 0)
    return value.astype(jnp.float32)


def kernel(
    shards,
    load_hbm,
    rack_hbm,
    pod_hbm,
    host_out,
    rack_out,
    pod_out,
    own,
    near,
    far,
    rack_ref,
    pod_ref,
    local_rack,
    partial,
    spill,
    totals,
    near_totals,
    far_totals,
    pod_terms,
    pod_in,
    pod_sum,
    slab_pods,
    rack_row,
    rack_row_in,
    host_row,
    host_row_in,
    load_sems,
    near_sems,
    far_send,
    far_recv,
    small_send,
    small_recv,
    pod_send,
    pod_recv,
):
    rows, hosts = own.shape
    racks = totals.shape[1]
    width = hosts // PARTS
    d = lax.axis_index("slab")
    h = lax.axis_index("hst")
    odd = lax.rem(d, 2)
    near_d = d + 1 - 2 * odd
    far_d = lax.rem(d + 3 + 2 * odd, SLABS)
    diag_d = lax.rem(d + 2, SLABS)
    window = 4 * SLAB_LEN + 1
    day = SLABS * rows

    barrier = pltpu.get_barrier_semaphore()
    for peer in (near_d, far_d, diag_d):
        pl.semaphore_signal(barrier, inc=1, device_id=(peer, h), device_id_type=MESH)

    @pl.loop(1, shards)
    def _(k):
        peer = lax.rem(h + k, shards)
        pl.semaphore_signal(barrier, inc=1, device_id=(d, peer), device_id_type=MESH)

    loads = [
        pltpu.make_async_copy(rack_hbm, rack_ref, load_sems.at[0]),
        pltpu.make_async_copy(pod_hbm, pod_ref, load_sems.at[1]),
        pltpu.make_async_copy(load_hbm, own, load_sems.at[2]),
    ]
    for copy in loads:
        copy.start()
    pl.semaphore_wait(barrier, SLABS - 1 + shards - 1)

    def far_copy(c):
        cols = pl.ds(pl.multiple_of(c * width, width), width)
        return pltpu.make_async_remote_copy(
            src_ref=load_hbm.at[:, cols],
            dst_ref=far.at[:, cols],
            send_sem=far_send.at[c],
            recv_sem=far_recv.at[c],
            device_id=(far_d, h),
            device_id_type=MESH,
        )

    def small_copy(src, dst, index, device):
        return pltpu.make_async_remote_copy(
            src_ref=src,
            dst_ref=dst,
            send_sem=small_send.at[index],
            recv_sem=small_recv.at[index],
            device_id=device,
            device_id_type=MESH,
        )

    for c in range(AHEAD):
        far_copy(c).start()
    near_copy = pltpu.make_async_remote_copy(
        src_ref=load_hbm,
        dst_ref=near,
        send_sem=near_sems.at[0],
        recv_sem=near_sems.at[1],
        device_id=(near_d, h),
        device_id_type=MESH,
    )
    near_copy.start()
    for copy in loads:
        copy.wait()
    local = rack_ref[...] - h * racks
    local_rack[...] = jnp.where(local < 0, local + racks * shards, local)

    def next_far(c):
        far_copy(c - AHEAD).wait_send()
        far_copy(c).start()

    partial[...] = jnp.zeros_like(partial)
    rack_ids = lax.broadcasted_iota(jnp.int32, (2 * racks, 128), 0)

    @pl.loop(0, PARTS)
    def _(c):
        cols = pl.ds(pl.multiple_of(c * width, width), width)
        member = jnp.concatenate(
            [
                (rack_ids == local_rack[pl.ds(c * (width // 128) + k, 1), :])
                .astype(jnp.float32)
                .astype(jnp.bfloat16)
                for k in range(width // 128)
            ],
            axis=1,
        )
        partial[...] += lax.dot_general(
            own[:, cols], member, NT, preferred_element_type=jnp.float32
        )

    spill_copy = small_copy(
        partial.at[:, pl.ds(racks, racks)], spill, 0, (d, lax.rem(h + 1, shards))
    )
    spill_copy.start()
    next_far(AHEAD)

    k_own = coefficients(d, d, rows, rows)
    k_near = coefficients(d, near_d, rows, rows)
    k_far = coefficients(d, far_d, rows, rows)
    k_diag = coefficients(diag_d, d, 8, rows)
    k_both = jnp.concatenate([k_own, k_diag], 0).astype(jnp.bfloat16)

    @pl.loop(0, PARTS)
    def _(c):
        cols = pl.ds(pl.multiple_of(c * width, width), width)
        both = jnp.dot(k_both, own[:, cols], preferred_element_type=jnp.float32)
        host_out[:, cols] = both[:rows]
        host_row[pl.ds(c, 1), :] = both[rows : rows + 1]

    host_row_copy = small_copy(host_row, host_row_in, 1, (diag_d, h))
    host_row_copy.start()

    spill_copy.wait()
    totals[...] = partial[:, :racks] + spill[...]
    slots = lax.broadcasted_iota(jnp.int32, (8 * shards, 128), 0)
    slot_pod = jnp.where(slots % 8 < POD_DEV, slots // 8 * POD_DEV + slots % 8, -1)
    pod_member = jnp.concatenate(
        [
            (slot_pod == pod_ref[pl.ds(k, 1), :]).astype(jnp.float32)
            for k in range(racks // 128)
        ],
        axis=1,
    )
    pod_terms[...] = lax.dot_general(
        pod_member, totals[...], NT, preferred_element_type=jnp.float32, precision=EXACT
    )

    def pod_copy(k):
        peer = lax.rem(h + k, shards)
        return pltpu.make_async_remote_copy(
            src_ref=pod_terms.at[pl.ds(pl.multiple_of(peer * 8, 8), 8), :],
            dst_ref=pod_in.at[k],
            send_sem=pod_send.at[k],
            recv_sem=pod_recv.at[k],
            device_id=(d, peer),
            device_id_type=MESH,
        )

    @pl.loop(1, shards)
    def _(k):
        pod_copy(k).start()

    rack_row[...] = jnp.dot(
        k_diag, totals[...], preferred_element_type=jnp.float32, precision=EXACT
    )
    copies = [
        small_copy(totals, far_totals, 2, (far_d, h)),
        small_copy(rack_row, rack_row_in, 3, (diag_d, h)),
        small_copy(totals, near_totals, 4, (near_d, h)),
    ]
    for copy in copies:
        copy.start()
    next_far(AHEAD + 1)

    near_copy.wait()
    k_near_half = k_near.astype(jnp.bfloat16)

    @pl.loop(0, PARTS)
    def _(c):
        cols = pl.ds(pl.multiple_of(c * width, width), width)
        host_out[:, cols] += jnp.dot(
            k_near_half, near[:, cols], preferred_element_type=jnp.float32
        )

    next_far(AHEAD + 2)
    pod_sum[...] = pod_terms[pl.ds(pl.multiple_of(h * 8, 8), 8), :]

    @pl.loop(1, shards)
    def _(k):
        pod_copy(k).wait()
        pod_sum[...] += pod_in[k]

    pod_copies = [
        small_copy(pod_sum, slab_pods.at[0], 5, (far_d, h)),
        small_copy(pod_sum, slab_pods.at[1], 6, (diag_d, h)),
        small_copy(pod_sum, slab_pods.at[2], 7, (near_d, h)),
    ]
    for copy in pod_copies:
        copy.start()

    host_row_copy.wait()
    k_far_half = k_far.astype(jnp.bfloat16)
    host_scale = 1.0 / (window * math.sqrt(day))

    def finish(c):
        cols = pl.ds(pl.multiple_of(c * width, width), width)
        far_copy(c).wait_recv()
        host_out[:, cols] = (
            host_out[:, cols]
            + jnp.dot(k_far_half, far[:, cols], preferred_element_type=jnp.float32)
            + host_row_in[pl.ds(c, 1), :]
        ) * host_scale

    for c in range(PARTS - 2):
        finish(c)
        if c + AHEAD + 3 < PARTS:
            next_far(c + AHEAD + 3)

    for copy in copies + pod_copies:
        copy.wait()

    def exact(a, b):
        return jnp.dot(a, b, preferred_element_type=jnp.float32, precision=EXACT)

    def exact_nt(a, b):
        return lax.dot_general(a, b, NT, preferred_element_type=jnp.float32, precision=EXACT)

    rack_scale = 1.0 / (window * math.sqrt(day * hosts / racks))
    rack_out[...] = (
        exact(k_own, totals[...])
        + exact(k_near, near_totals[...])
        + exact(k_far, far_totals[...])
        + rack_row_in[0:1, :]
    ) * rack_scale
    pod_scale = 1.0 / (window * math.sqrt(day * hosts / POD_DEV))
    pods = (
        exact_nt(pod_sum[...], k_own)
        + exact_nt(slab_pods[0], k_far)
        + exact_nt(slab_pods[1], coefficients(d, diag_d, rows, rows))
        + exact_nt(slab_pods[2], k_near)
    ) * pod_scale
    pod_out[...] = pods[:POD_DEV]

    for c in range(PARTS - 2, PARTS):
        finish(c)
    for c in range(PARTS - AHEAD, PARTS):
        far_copy(c).wait_send()


def write_out(host, rack, pod, host_out, rack_out, pod_out, sems):
    rows = host.shape[0]
    copies = [
        pltpu.make_async_copy(
            host.at[pl.ds(8 * k, 8), :], host_out.at[pl.ds(8 * k, 8), :], sems.at[k]
        )
        for k in range(rows // 8)
    ]
    copies.append(pltpu.make_async_copy(rack, rack_out, sems.at[rows // 8]))
    copies.append(pltpu.make_async_copy(pod, pod_out, sems.at[rows // 8 + 1]))
    for copy in copies:
        copy.start()
    for copy in copies:
        copy.wait()


def on_device(load, host_rack, rack_pod):
    rows, hosts = load.shape
    racks = rack_pod.shape[0]
    shards = lax.axis_size("hst")
    f32 = jnp.float32
    vmem = pl.BlockSpec(memory_space=pltpu.VMEM)
    hbm = pl.BlockSpec(memory_space=pltpu.HBM)
    shapes = (
        jax.ShapeDtypeStruct((rows, hosts), f32),
        jax.ShapeDtypeStruct((rows, racks), f32),
        jax.ShapeDtypeStruct((POD_DEV, rows), f32),
    )
    results = pl.pallas_call(
        functools.partial(kernel, shards),
        out_shape=shapes,
        in_specs=[hbm, hbm, hbm],
        out_specs=(vmem, vmem, vmem),
        scratch_shapes=[
            pltpu.VMEM((rows, hosts), load.dtype),
            pltpu.VMEM((rows, hosts), load.dtype),
            pltpu.VMEM((rows, hosts), load.dtype),
            pltpu.VMEM((hosts // 128, 128), jnp.int32),
            pltpu.VMEM((racks // 128, 128), jnp.int32),
            pltpu.VMEM((hosts // 128, 128), jnp.int32),
            pltpu.VMEM((rows, 2 * racks), f32),
            pltpu.VMEM((rows, racks), f32),
            pltpu.VMEM((rows, racks), f32),
            pltpu.VMEM((rows, racks), f32),
            pltpu.VMEM((rows, racks), f32),
            pltpu.VMEM((8 * shards, rows), f32),
            pltpu.VMEM((shards, 8, rows), f32),
            pltpu.VMEM((8, rows), f32),
            pltpu.VMEM((SLABS - 1, 8, rows), f32),
            pltpu.VMEM((8, racks), f32),
            pltpu.VMEM((8, racks), f32),
            pltpu.VMEM((PARTS, hosts // PARTS), f32),
            pltpu.VMEM((PARTS, hosts // PARTS), f32),
            pltpu.SemaphoreType.DMA((3,)),
            pltpu.SemaphoreType.DMA((2,)),
            pltpu.SemaphoreType.DMA((PARTS,)),
            pltpu.SemaphoreType.DMA((PARTS,)),
            pltpu.SemaphoreType.DMA((8,)),
            pltpu.SemaphoreType.DMA((8,)),
            pltpu.SemaphoreType.DMA((shards,)),
            pltpu.SemaphoreType.DMA((shards,)),
        ],
        compiler_params=pltpu.CompilerParams(
            collective_id=0, has_side_effects=True, vmem_limit_bytes=40 * 1024 * 1024
        ),
        cost_estimate=pl.CostEstimate(
            flops=2 * rows * hosts * (3 * rows + 2 * racks),
            bytes_accessed=rows * hosts * 10,
            transcendentals=0,
        ),
    )(load, host_rack.reshape(hosts // 128, 128), rack_pod.reshape(racks // 128, 128))
    host, rack, pod = pl.pallas_call(
        write_out,
        out_shape=shapes,
        in_specs=[vmem, vmem, vmem],
        out_specs=(hbm, hbm, hbm),
        scratch_shapes=[pltpu.SemaphoreType.DMA((rows // 8 + 2,))],
    )(*results)
    return host, rack, pod.T


def solution(mesh):
    in_specs = (P("slab", "hst"), P("hst"), P("hst"))
    out_specs = (P("slab", "hst"), P("slab", "hst"), P("slab", "hst"))
    return jax.shard_map(
        on_device, mesh=mesh, in_specs=in_specs, out_specs=out_specs, check_vma=False
    )
```

```python
import functools
import math

import jax
import jax.numpy as jnp
from jax import lax
from jax.experimental import pallas as pl
from jax.experimental.pallas import tpu as pltpu
from jax.sharding import PartitionSpec as P

SLAB_LEN = 36
POD_DEV = 2
SLABS = 4
PARTS = 8
AHEAD = 3
MESH = pl.DeviceIdType.MESH
EXACT = lax.Precision.HIGHEST
NT = (((1,), (1,)), ((), ()))


def coefficients(target, source, out_rows, rows):
    reach = 2 * SLAB_LEN
    day = SLABS * rows
    t = target * rows + lax.broadcasted_iota(jnp.int32, (out_rows, rows), 0)
    u = source * rows + lax.broadcasted_iota(jnp.int32, (out_rows, rows), 1)
    value = jnp.where(u <= t, 2 * reach + 1, 0)
    for wrap in (-day, 0, day):
        first = jnp.maximum(u + (wrap - reach), 0)
        last = jnp.minimum(u + (wrap + reach), t)
        value = value - jnp.maximum(last - first + 1, 0)
    return value.astype(jnp.float32)


def kernel(
    shards,
    load_hbm,
    rack_hbm,
    pod_hbm,
    host_hbm,
    rack_out_hbm,
    pod_out_hbm,
    host_out,
    rack_out,
    pod_out,
    own,
    near,
    far,
    rack_ref,
    pod_ref,
    local_rack,
    partial,
    spill,
    totals,
    near_totals,
    far_totals,
    pod_terms,
    pod_in,
    pod_sum,
    slab_pods,
    rack_row,
    rack_row_in,
    host_row,
    host_row_in,
    load_sems,
    near_sems,
    far_send,
    far_recv,
    small_send,
    small_recv,
    pod_send,
    pod_recv,
    out_sems,
):
    rows, hosts = own.shape
    racks = totals.shape[1]
    width = hosts // PARTS
    d = lax.axis_index("slab")
    h = lax.axis_index("hst")
    odd = lax.rem(d, 2)
    near_d = d + 1 - 2 * odd
    far_d = lax.rem(d + 3 + 2 * odd, SLABS)
    diag_d = lax.rem(d + 2, SLABS)
    window = 4 * SLAB_LEN + 1
    day = SLABS * rows

    barrier = pltpu.get_barrier_semaphore()
    for peer in (near_d, far_d, diag_d):
        pl.semaphore_signal(barrier, inc=1, device_id=(peer, h), device_id_type=MESH)

    @pl.loop(1, shards)
    def _(k):
        peer = lax.rem(h + k, shards)
        pl.semaphore_signal(barrier, inc=1, device_id=(d, peer), device_id_type=MESH)

    loads = [
        pltpu.make_async_copy(rack_hbm, rack_ref, load_sems.at[0]),
        pltpu.make_async_copy(pod_hbm, pod_ref, load_sems.at[1]),
        pltpu.make_async_copy(load_hbm, own, load_sems.at[2]),
    ]
    for copy in loads:
        copy.start()
    pl.semaphore_wait(barrier, SLABS - 1 + shards - 1)

    def far_copy(c):
        cols = pl.ds(pl.multiple_of(c * width, width), width)
        return pltpu.make_async_remote_copy(
            src_ref=load_hbm.at[:, cols],
            dst_ref=far.at[:, cols],
            send_sem=far_send.at[c],
            recv_sem=far_recv.at[c],
            device_id=(far_d, h),
            device_id_type=MESH,
        )

    def small_copy(src, dst, index, device):
        return pltpu.make_async_remote_copy(
            src_ref=src,
            dst_ref=dst,
            send_sem=small_send.at[index],
            recv_sem=small_recv.at[index],
            device_id=device,
            device_id_type=MESH,
        )

    for c in range(AHEAD):
        far_copy(c).start()
    near_copy = pltpu.make_async_remote_copy(
        src_ref=load_hbm,
        dst_ref=near,
        send_sem=near_sems.at[0],
        recv_sem=near_sems.at[1],
        device_id=(near_d, h),
        device_id_type=MESH,
    )
    near_copy.start()
    for copy in loads:
        copy.wait()
    local = rack_ref[...] - h * racks
    local_rack[...] = jnp.where(local < 0, local + racks * shards, local)

    def next_far(c):
        far_copy(c - AHEAD).wait_send()
        far_copy(c).start()

    partial[...] = jnp.zeros_like(partial)
    rack_ids = lax.broadcasted_iota(jnp.int32, (2 * racks, 128), 0)

    @pl.loop(0, PARTS)
    def _(c):
        cols = pl.ds(pl.multiple_of(c * width, width), width)
        member = jnp.concatenate(
            [
                (rack_ids == local_rack[pl.ds(c * (width // 128) + k, 1), :])
                .astype(jnp.float32)
                .astype(jnp.bfloat16)
                for k in range(width // 128)
            ],
            axis=1,
        )
        partial[...] += lax.dot_general(
            own[:, cols], member, NT, preferred_element_type=jnp.float32
        )

    spill_copy = small_copy(
        partial.at[:, pl.ds(racks, racks)], spill, 0, (d, lax.rem(h + 1, shards))
    )
    spill_copy.start()
    next_far(AHEAD)

    k_own = coefficients(d, d, rows, rows)
    k_near = coefficients(d, near_d, rows, rows)
    k_far = coefficients(d, far_d, rows, rows)
    k_diag = coefficients(diag_d, d, 8, rows)
    k_both = jnp.concatenate([k_own, k_diag], 0).astype(jnp.bfloat16)

    @pl.loop(0, PARTS)
    def _(c):
        cols = pl.ds(pl.multiple_of(c * width, width), width)
        both = jnp.dot(k_both, own[:, cols], preferred_element_type=jnp.float32)
        host_out[:, cols] = both[:rows]
        host_row[pl.ds(c, 1), :] = both[rows : rows + 1]

    host_row_copy = small_copy(host_row, host_row_in, 1, (diag_d, h))
    host_row_copy.start()

    spill_copy.wait()
    totals[...] = partial[:, :racks] + spill[...]
    slots = lax.broadcasted_iota(jnp.int32, (8 * shards, 128), 0)
    slot_pod = jnp.where(slots % 8 < POD_DEV, slots // 8 * POD_DEV + slots % 8, -1)
    pod_member = jnp.concatenate(
        [
            (slot_pod == pod_ref[pl.ds(k, 1), :]).astype(jnp.float32)
            for k in range(racks // 128)
        ],
        axis=1,
    )
    pod_terms[...] = lax.dot_general(
        pod_member, totals[...], NT, preferred_element_type=jnp.float32, precision=EXACT
    )

    def pod_copy(k):
        peer = lax.rem(h + k, shards)
        return pltpu.make_async_remote_copy(
            src_ref=pod_terms.at[pl.ds(pl.multiple_of(peer * 8, 8), 8), :],
            dst_ref=pod_in.at[k],
            send_sem=pod_send.at[k],
            recv_sem=pod_recv.at[k],
            device_id=(d, peer),
            device_id_type=MESH,
        )

    @pl.loop(1, shards)
    def _(k):
        pod_copy(k).start()

    rack_row[...] = jnp.dot(
        k_diag, totals[...], preferred_element_type=jnp.float32, precision=EXACT
    )
    copies = [
        small_copy(totals, far_totals, 2, (far_d, h)),
        small_copy(rack_row, rack_row_in, 3, (diag_d, h)),
        small_copy(totals, near_totals, 4, (near_d, h)),
    ]
    for copy in copies:
        copy.start()
    next_far(AHEAD + 1)

    near_copy.wait()
    k_near_half = k_near.astype(jnp.bfloat16)

    @pl.loop(0, PARTS)
    def _(c):
        cols = pl.ds(pl.multiple_of(c * width, width), width)
        host_out[:, cols] += jnp.dot(
            k_near_half, near[:, cols], preferred_element_type=jnp.float32
        )

    next_far(AHEAD + 2)
    pod_sum[...] = pod_terms[pl.ds(pl.multiple_of(h * 8, 8), 8), :]

    @pl.loop(1, shards)
    def _(k):
        pod_copy(k).wait()
        pod_sum[...] += pod_in[k]

    pod_copies = [
        small_copy(pod_sum, slab_pods.at[0], 5, (far_d, h)),
        small_copy(pod_sum, slab_pods.at[1], 6, (diag_d, h)),
        small_copy(pod_sum, slab_pods.at[2], 7, (near_d, h)),
    ]
    for copy in pod_copies:
        copy.start()

    host_row_copy.wait()
    k_far_half = k_far.astype(jnp.bfloat16)
    host_scale = 1.0 / (window * math.sqrt(day))

    def out_copy(c):
        cols = pl.ds(pl.multiple_of(c * width, width), width)
        return pltpu.make_async_copy(host_out.at[:, cols], host_hbm.at[:, cols], out_sems.at[c])

    def finish(c):
        cols = pl.ds(pl.multiple_of(c * width, width), width)
        far_copy(c).wait_recv()
        host_out[:, cols] = (
            host_out[:, cols]
            + jnp.dot(k_far_half, far[:, cols], preferred_element_type=jnp.float32)
            + host_row_in[pl.ds(c, 1), :]
        ) * host_scale
        out_copy(c).start()

    for c in range(PARTS - 2):
        finish(c)
        if c + AHEAD + 3 < PARTS:
            next_far(c + AHEAD + 3)

    for copy in copies + pod_copies:
        copy.wait()

    def exact(a, b):
        return jnp.dot(a, b, preferred_element_type=jnp.float32, precision=EXACT)

    def exact_nt(a, b):
        return lax.dot_general(a, b, NT, preferred_element_type=jnp.float32, precision=EXACT)

    rack_scale = 1.0 / (window * math.sqrt(day * hosts / racks))
    rack_out[...] = (
        exact(k_own, totals[...])
        + exact(k_near, near_totals[...])
        + exact(k_far, far_totals[...])
        + rack_row_in[0:1, :]
    ) * rack_scale
    pod_scale = 1.0 / (window * math.sqrt(day * hosts / POD_DEV))
    pods = (
        exact_nt(pod_sum[...], k_own)
        + exact_nt(slab_pods[0], k_far)
        + exact_nt(slab_pods[1], coefficients(d, diag_d, rows, rows))
        + exact_nt(slab_pods[2], k_near)
    ) * pod_scale
    pod_out[...] = pods[:POD_DEV]
    group_copies = [
        pltpu.make_async_copy(rack_out, rack_out_hbm, out_sems.at[PARTS]),
        pltpu.make_async_copy(pod_out, pod_out_hbm, out_sems.at[PARTS + 1]),
    ]
    for copy in group_copies:
        copy.start()

    for c in range(PARTS - 2, PARTS):
        finish(c)
    for c in range(PARTS - AHEAD, PARTS):
        far_copy(c).wait_send()
    for copy in group_copies:
        copy.wait()
    for c in range(PARTS):
        out_copy(c).wait()


def on_device(load, host_rack, rack_pod):
    rows, hosts = load.shape
    racks = rack_pod.shape[0]
    shards = lax.axis_size("hst")
    f32 = jnp.float32
    hbm = pl.BlockSpec(memory_space=pltpu.HBM)
    shapes = (
        jax.ShapeDtypeStruct((rows, hosts), f32),
        jax.ShapeDtypeStruct((rows, racks), f32),
        jax.ShapeDtypeStruct((POD_DEV, rows), f32),
    )
    host, rack, pod = pl.pallas_call(
        functools.partial(kernel, shards),
        out_shape=shapes,
        in_specs=[hbm, hbm, hbm],
        out_specs=(hbm, hbm, hbm),
        scratch_shapes=[
            pltpu.VMEM((rows, hosts), f32),
            pltpu.VMEM((rows, racks), f32),
            pltpu.VMEM((POD_DEV, rows), f32),
            pltpu.VMEM((rows, hosts), load.dtype),
            pltpu.VMEM((rows, hosts), load.dtype),
            pltpu.VMEM((rows, hosts), load.dtype),
            pltpu.VMEM((hosts // 128, 128), jnp.int32),
            pltpu.VMEM((racks // 128, 128), jnp.int32),
            pltpu.VMEM((hosts // 128, 128), jnp.int32),
            pltpu.VMEM((rows, 2 * racks), f32),
            pltpu.VMEM((rows, racks), f32),
            pltpu.VMEM((rows, racks), f32),
            pltpu.VMEM((rows, racks), f32),
            pltpu.VMEM((rows, racks), f32),
            pltpu.VMEM((8 * shards, rows), f32),
            pltpu.VMEM((shards, 8, rows), f32),
            pltpu.VMEM((8, rows), f32),
            pltpu.VMEM((SLABS - 1, 8, rows), f32),
            pltpu.VMEM((8, racks), f32),
            pltpu.VMEM((8, racks), f32),
            pltpu.VMEM((PARTS, hosts // PARTS), f32),
            pltpu.VMEM((PARTS, hosts // PARTS), f32),
            pltpu.SemaphoreType.DMA((3,)),
            pltpu.SemaphoreType.DMA((2,)),
            pltpu.SemaphoreType.DMA((PARTS,)),
            pltpu.SemaphoreType.DMA((PARTS,)),
            pltpu.SemaphoreType.DMA((8,)),
            pltpu.SemaphoreType.DMA((8,)),
            pltpu.SemaphoreType.DMA((shards,)),
            pltpu.SemaphoreType.DMA((shards,)),
            pltpu.SemaphoreType.DMA((PARTS + 2,)),
        ],
        compiler_params=pltpu.CompilerParams(
            collective_id=0, has_side_effects=True
        ),
        cost_estimate=pl.CostEstimate(
            flops=2 * rows * hosts * (3 * rows + 2 * racks),
            bytes_accessed=rows * hosts * 10,
            transcendentals=0,
        ),
    )(load, host_rack.reshape(hosts // 128, 128), rack_pod.reshape(racks // 128, 128))
    return host, rack, pod.T


def solution(mesh):
    in_specs = (P("slab", "hst"), P("hst"), P("hst"))
    out_specs = (P("slab", "hst"), P("slab", "hst"), P("slab", "hst"))
    return jax.shard_map(
        on_device, mesh=mesh, in_specs=in_specs, out_specs=out_specs, check_vma=False
    )
```

```python
import functools
import math

import jax
import jax.numpy as jnp
from jax import lax
from jax.experimental import pallas as pl
from jax.experimental.pallas import tpu as pltpu
from jax.sharding import PartitionSpec as P

SLAB_LEN = 36
POD_DEV = 2
SLABS = 4
PARTS = 8
AHEAD = 3
MESH = pl.DeviceIdType.MESH
EXACT = lax.Precision.HIGHEST
NT = (((1,), (1,)), ((), ()))


def coefficients(target, source, out_rows, rows):
    reach = 2 * SLAB_LEN
    day = SLABS * rows
    t = target * rows + lax.broadcasted_iota(jnp.int32, (out_rows, rows), 0)
    u = source * rows + lax.broadcasted_iota(jnp.int32, (out_rows, rows), 1)
    value = jnp.where(u <= t, 2 * reach + 1, 0)
    for wrap in (-day, 0, day):
        first = jnp.maximum(u + (wrap - reach), 0)
        last = jnp.minimum(u + (wrap + reach), t)
        value = value - jnp.maximum(last - first + 1, 0)
    return value.astype(jnp.float32)


def kernel(
    shards,
    load_hbm,
    rack_hbm,
    pod_hbm,
    host_out,
    rack_out,
    pod_out,
    own,
    near,
    far,
    rack_ref,
    pod_ref,
    local_rack,
    partial,
    spill,
    totals,
    near_totals,
    far_totals,
    pod_terms,
    pod_in,
    pod_sum,
    slab_pods,
    rack_row,
    rack_row_in,
    host_row,
    host_row_in,
    load_sems,
    near_sems,
    far_send,
    far_recv,
    small_send,
    small_recv,
    pod_send,
    pod_recv,
):
    rows, hosts = own.shape
    racks = totals.shape[1]
    width = hosts // PARTS
    d = lax.axis_index("slab")
    h = lax.axis_index("hst")
    odd = lax.rem(d, 2)
    near_d = d + 1 - 2 * odd
    far_d = lax.rem(d + 3 + 2 * odd, SLABS)
    diag_d = lax.rem(d + 2, SLABS)
    window = 4 * SLAB_LEN + 1
    day = SLABS * rows

    barrier = pltpu.get_barrier_semaphore()
    for peer in (near_d, far_d, diag_d):
        pl.semaphore_signal(barrier, inc=1, device_id=(peer, h), device_id_type=MESH)

    @pl.loop(1, shards)
    def _(k):
        peer = lax.rem(h + k, shards)
        pl.semaphore_signal(barrier, inc=1, device_id=(d, peer), device_id_type=MESH)

    loads = [
        pltpu.make_async_copy(rack_hbm, rack_ref, load_sems.at[0]),
        pltpu.make_async_copy(pod_hbm, pod_ref, load_sems.at[1]),
        pltpu.make_async_copy(load_hbm, own, load_sems.at[2]),
    ]
    for copy in loads:
        copy.start()
    pl.semaphore_wait(barrier, SLABS - 1 + shards - 1)

    def far_copy(c):
        cols = pl.ds(pl.multiple_of(c * width, width), width)
        return pltpu.make_async_remote_copy(
            src_ref=load_hbm.at[:, cols],
            dst_ref=far.at[:, cols],
            send_sem=far_send.at[c],
            recv_sem=far_recv.at[c],
            device_id=(far_d, h),
            device_id_type=MESH,
        )

    def small_copy(src, dst, index, device):
        return pltpu.make_async_remote_copy(
            src_ref=src,
            dst_ref=dst,
            send_sem=small_send.at[index],
            recv_sem=small_recv.at[index],
            device_id=device,
            device_id_type=MESH,
        )

    for c in range(AHEAD):
        far_copy(c).start()
    near_copy = pltpu.make_async_remote_copy(
        src_ref=load_hbm,
        dst_ref=near,
        send_sem=near_sems.at[0],
        recv_sem=near_sems.at[1],
        device_id=(near_d, h),
        device_id_type=MESH,
    )
    near_copy.start()
    for copy in loads:
        copy.wait()
    local = rack_ref[...] - h * racks
    local_rack[...] = jnp.where(local < 0, local + racks * shards, local)

    def next_far(c):
        far_copy(c - AHEAD).wait_send()
        far_copy(c).start()

    partial[...] = jnp.zeros_like(partial)
    rack_ids = lax.broadcasted_iota(jnp.int32, (2 * racks, 128), 0)

    @pl.loop(0, PARTS)
    def _(c):
        cols = pl.ds(pl.multiple_of(c * width, width), width)
        member = jnp.concatenate(
            [
                (rack_ids == local_rack[pl.ds(c * (width // 128) + k, 1), :])
                .astype(jnp.float32)
                .astype(jnp.bfloat16)
                for k in range(width // 128)
            ],
            axis=1,
        )
        partial[...] += lax.dot_general(
            own[:, cols], member, NT, preferred_element_type=jnp.float32
        )

    spill_copy = small_copy(
        partial.at[:, pl.ds(racks, racks)], spill, 0, (d, lax.rem(h + 1, shards))
    )
    spill_copy.start()
    next_far(AHEAD)

    k_own = coefficients(d, d, rows, rows)
    k_near = coefficients(d, near_d, rows, rows)
    k_far = coefficients(d, far_d, rows, rows)
    k_diag = coefficients(diag_d, d, 8, rows)
    k_both = jnp.concatenate([k_own, k_diag], 0).astype(jnp.bfloat16)

    @pl.loop(0, PARTS)
    def _(c):
        cols = pl.ds(pl.multiple_of(c * width, width), width)
        both = jnp.dot(k_both, own[:, cols], preferred_element_type=jnp.float32)
        host_out[:, cols] = both[:rows]
        host_row[pl.ds(c, 1), :] = both[rows : rows + 1]

    host_row_copy = small_copy(host_row, host_row_in, 1, (diag_d, h))
    host_row_copy.start()

    spill_copy.wait()
    totals[...] = partial[:, :racks] + spill[...]
    slots = lax.broadcasted_iota(jnp.int32, (8 * shards, 128), 0)
    slot_pod = jnp.where(slots % 8 < POD_DEV, slots // 8 * POD_DEV + slots % 8, -1)
    pod_member = jnp.concatenate(
        [
            (slot_pod == pod_ref[pl.ds(k, 1), :]).astype(jnp.float32)
            for k in range(racks // 128)
        ],
        axis=1,
    )
    pod_terms[...] = lax.dot_general(
        pod_member, totals[...], NT, preferred_element_type=jnp.float32, precision=EXACT
    )

    def pod_copy(k):
        peer = lax.rem(h + k, shards)
        return pltpu.make_async_remote_copy(
            src_ref=pod_terms.at[pl.ds(pl.multiple_of(peer * 8, 8), 8), :],
            dst_ref=pod_in.at[k],
            send_sem=pod_send.at[k],
            recv_sem=pod_recv.at[k],
            device_id=(d, peer),
            device_id_type=MESH,
        )

    @pl.loop(1, shards)
    def _(k):
        pod_copy(k).start()

    rack_row[...] = jnp.dot(
        k_diag, totals[...], preferred_element_type=jnp.float32, precision=EXACT
    )
    copies = [
        small_copy(totals, far_totals, 2, (far_d, h)),
        small_copy(rack_row, rack_row_in, 3, (diag_d, h)),
        small_copy(totals, near_totals, 4, (near_d, h)),
    ]
    for copy in copies:
        copy.start()
    next_far(AHEAD + 1)

    near_copy.wait()
    k_near_half = k_near.astype(jnp.bfloat16)

    @pl.loop(0, PARTS)
    def _(c):
        cols = pl.ds(pl.multiple_of(c * width, width), width)
        host_out[:, cols] += jnp.dot(
            k_near_half, near[:, cols], preferred_element_type=jnp.float32
        )

    next_far(AHEAD + 2)
    pod_sum[...] = pod_terms[pl.ds(pl.multiple_of(h * 8, 8), 8), :]

    @pl.loop(1, shards)
    def _(k):
        pod_copy(k).wait()
        pod_sum[...] += pod_in[k]

    pod_copies = [
        small_copy(pod_sum, slab_pods.at[0], 5, (far_d, h)),
        small_copy(pod_sum, slab_pods.at[1], 6, (diag_d, h)),
        small_copy(pod_sum, slab_pods.at[2], 7, (near_d, h)),
    ]
    for copy in pod_copies:
        copy.start()

    host_row_copy.wait()
    k_far_half = k_far.astype(jnp.bfloat16)
    host_scale = 1.0 / (window * math.sqrt(day))

    def finish(c):
        cols = pl.ds(pl.multiple_of(c * width, width), width)
        far_copy(c).wait_recv()
        host_out[:, cols] = (
            host_out[:, cols]
            + jnp.dot(k_far_half, far[:, cols], preferred_element_type=jnp.float32)
            + host_row_in[pl.ds(c, 1), :]
        ) * host_scale

    for c in range(PARTS - 2):
        finish(c)
        if c + AHEAD + 3 < PARTS:
            next_far(c + AHEAD + 3)

    for copy in copies + pod_copies:
        copy.wait()

    def exact(a, b):
        return jnp.dot(a, b, preferred_element_type=jnp.float32, precision=EXACT)

    def exact_nt(a, b):
        return lax.dot_general(a, b, NT, preferred_element_type=jnp.float32, precision=EXACT)

    rack_scale = 1.0 / (window * math.sqrt(day * hosts / racks))
    rack_out[...] = (
        exact(k_own, totals[...])
        + exact(k_near, near_totals[...])
        + exact(k_far, far_totals[...])
        + rack_row_in[0:1, :]
    ) * rack_scale
    pod_scale = 1.0 / (window * math.sqrt(day * hosts / POD_DEV))
    pods = (
        exact_nt(pod_sum[...], k_own)
        + exact_nt(slab_pods[0], k_far)
        + exact_nt(slab_pods[1], coefficients(d, diag_d, rows, rows))
        + exact_nt(slab_pods[2], k_near)
    ) * pod_scale
    pod_out[...] = pods[:POD_DEV]

    for c in range(PARTS - 2, PARTS):
        finish(c)
    for c in range(PARTS - AHEAD, PARTS):
        far_copy(c).wait_send()


def on_device(load, host_rack, rack_pod):
    rows, hosts = load.shape
    racks = rack_pod.shape[0]
    shards = lax.axis_size("hst")
    f32 = jnp.float32
    hbm = pl.BlockSpec(memory_space=pltpu.HBM)
    vmem = pl.BlockSpec(memory_space=pltpu.VMEM)
    shapes = (
        pltpu.VMEM((rows, hosts), f32),
        pltpu.VMEM((rows, racks), f32),
        pltpu.VMEM((POD_DEV, rows), f32),
    )
    placed = functools.partial(pltpu.with_memory_space_constraint, memory_space=pltpu.HBM)
    host, rack, pod = pl.pallas_call(
        functools.partial(kernel, shards),
        out_shape=shapes,
        in_specs=[hbm, hbm, hbm],
        out_specs=(vmem, vmem, vmem),
        scratch_shapes=[
            pltpu.VMEM((rows, hosts), load.dtype),
            pltpu.VMEM((rows, hosts), load.dtype),
            pltpu.VMEM((rows, hosts), load.dtype),
            pltpu.VMEM((hosts // 128, 128), jnp.int32),
            pltpu.VMEM((racks // 128, 128), jnp.int32),
            pltpu.VMEM((hosts // 128, 128), jnp.int32),
            pltpu.VMEM((rows, 2 * racks), f32),
            pltpu.VMEM((rows, racks), f32),
            pltpu.VMEM((rows, racks), f32),
            pltpu.VMEM((rows, racks), f32),
            pltpu.VMEM((rows, racks), f32),
            pltpu.VMEM((8 * shards, rows), f32),
            pltpu.VMEM((shards, 8, rows), f32),
            pltpu.VMEM((8, rows), f32),
            pltpu.VMEM((SLABS - 1, 8, rows), f32),
            pltpu.VMEM((8, racks), f32),
            pltpu.VMEM((8, racks), f32),
            pltpu.VMEM((PARTS, hosts // PARTS), f32),
            pltpu.VMEM((PARTS, hosts // PARTS), f32),
            pltpu.SemaphoreType.DMA((3,)),
            pltpu.SemaphoreType.DMA((2,)),
            pltpu.SemaphoreType.DMA((PARTS,)),
            pltpu.SemaphoreType.DMA((PARTS,)),
            pltpu.SemaphoreType.DMA((8,)),
            pltpu.SemaphoreType.DMA((8,)),
            pltpu.SemaphoreType.DMA((shards,)),
            pltpu.SemaphoreType.DMA((shards,)),
        ],
        compiler_params=pltpu.CompilerParams(
            collective_id=0, has_side_effects=True, vmem_limit_bytes=40 * 1024 * 1024
        ),
        cost_estimate=pl.CostEstimate(
            flops=2 * rows * hosts * (3 * rows + 2 * racks),
            bytes_accessed=rows * hosts * 10,
            transcendentals=0,
        ),
    )(
        placed(load),
        placed(host_rack.reshape(hosts // 128, 128)),
        placed(rack_pod.reshape(racks // 128, 128)),
    )
    return host, rack, pod.T


def solution(mesh):
    in_specs = (P("slab", "hst"), P("hst"), P("hst"))
    out_specs = (P("slab", "hst"), P("slab", "hst"), P("slab", "hst"))
    return jax.shard_map(
        on_device, mesh=mesh, in_specs=in_specs, out_specs=out_specs, check_vma=False
    )
```

```python
import functools
import math

import jax
import jax.numpy as jnp
from jax import lax
from jax.experimental import pallas as pl
from jax.experimental.pallas import tpu as pltpu
from jax.sharding import PartitionSpec as P

SLAB_LEN = 36
POD_DEV = 2
SLABS = 4
PARTS = 8
AHEAD = 5
MESH = pl.DeviceIdType.MESH
EXACT = lax.Precision.HIGHEST
NT = (((1,), (1,)), ((), ()))


def coefficients(target, source, out_rows, rows):
    reach = 2 * SLAB_LEN
    day = SLABS * rows
    t = target * rows + lax.broadcasted_iota(jnp.int32, (out_rows, rows), 0)
    u = source * rows + lax.broadcasted_iota(jnp.int32, (out_rows, rows), 1)
    value = jnp.where(u <= t, 2 * reach + 1, 0)
    for wrap in (-day, 0, day):
        first = jnp.maximum(u + (wrap - reach), 0)
        last = jnp.minimum(u + (wrap + reach), t)
        value = value - jnp.maximum(last - first + 1, 0)
    return value.astype(jnp.float32)


def kernel(
    shards,
    load_hbm,
    rack_hbm,
    pod_hbm,
    host_out,
    rack_out,
    pod_out,
    own,
    near,
    far,
    rack_ref,
    pod_ref,
    local_rack,
    partial,
    spill,
    totals,
    near_totals,
    far_totals,
    pod_terms,
    pod_in,
    pod_sum,
    slab_pods,
    rack_row,
    rack_row_in,
    host_row,
    host_row_in,
    load_sems,
    near_sems,
    far_send,
    far_recv,
    small_send,
    small_recv,
    pod_send,
    pod_recv,
):
    rows, hosts = own.shape
    racks = totals.shape[1]
    width = hosts // PARTS
    d = lax.axis_index("slab")
    h = lax.axis_index("hst")
    odd = lax.rem(d, 2)
    near_d = d + 1 - 2 * odd
    far_d = lax.rem(d + 3 + 2 * odd, SLABS)
    diag_d = lax.rem(d + 2, SLABS)
    window = 4 * SLAB_LEN + 1
    day = SLABS * rows

    barrier = pltpu.get_barrier_semaphore()
    for peer in (near_d, far_d, diag_d):
        pl.semaphore_signal(barrier, inc=1, device_id=(peer, h), device_id_type=MESH)

    @pl.loop(1, shards)
    def _(k):
        peer = lax.rem(h + k, shards)
        pl.semaphore_signal(barrier, inc=1, device_id=(d, peer), device_id_type=MESH)

    loads = [
        pltpu.make_async_copy(rack_hbm, rack_ref, load_sems.at[0]),
        pltpu.make_async_copy(pod_hbm, pod_ref, load_sems.at[1]),
        pltpu.make_async_copy(load_hbm, own, load_sems.at[2]),
    ]
    for copy in loads:
        copy.start()
    pl.semaphore_wait(barrier, SLABS - 1 + shards - 1)

    def far_copy(c):
        cols = pl.ds(pl.multiple_of(c * width, width), width)
        return pltpu.make_async_remote_copy(
            src_ref=load_hbm.at[:, cols],
            dst_ref=far.at[:, cols],
            send_sem=far_send.at[c],
            recv_sem=far_recv.at[c],
            device_id=(far_d, h),
            device_id_type=MESH,
        )

    def small_copy(src, dst, index, device):
        return pltpu.make_async_remote_copy(
            src_ref=src,
            dst_ref=dst,
            send_sem=small_send.at[index],
            recv_sem=small_recv.at[index],
            device_id=device,
            device_id_type=MESH,
        )

    for c in range(AHEAD):
        far_copy(c).start()
    near_copy = pltpu.make_async_remote_copy(
        src_ref=load_hbm,
        dst_ref=near,
        send_sem=near_sems.at[0],
        recv_sem=near_sems.at[1],
        device_id=(near_d, h),
        device_id_type=MESH,
    )
    near_copy.start()
    for copy in loads:
        copy.wait()
    local = rack_ref[...] - h * racks
    local_rack[...] = jnp.where(local < 0, local + racks * shards, local)

    def next_far(c):
        far_copy(c - AHEAD).wait_send()
        far_copy(c).start()

    partial[...] = jnp.zeros_like(partial)
    rack_ids = lax.broadcasted_iota(jnp.int32, (2 * racks, 128), 0)

    @pl.loop(0, PARTS)
    def _(c):
        cols = pl.ds(pl.multiple_of(c * width, width), width)
        member = jnp.concatenate(
            [
                (rack_ids == local_rack[pl.ds(c * (width // 128) + k, 1), :])
                .astype(jnp.float32)
                .astype(jnp.bfloat16)
                for k in range(width // 128)
            ],
            axis=1,
        )
        partial[...] += lax.dot_general(
            own[:, cols], member, NT, preferred_element_type=jnp.float32
        )

    spill_copy = small_copy(
        partial.at[:, pl.ds(racks, racks)], spill, 0, (d, lax.rem(h + 1, shards))
    )
    spill_copy.start()
    next_far(AHEAD)

    k_own = coefficients(d, d, rows, rows)
    k_near = coefficients(d, near_d, rows, rows)
    k_far = coefficients(d, far_d, rows, rows)
    k_diag = coefficients(diag_d, d, 8, rows)
    k_both = jnp.concatenate([k_own, k_diag], 0).astype(jnp.bfloat16)

    @pl.loop(0, PARTS)
    def _(c):
        cols = pl.ds(pl.multiple_of(c * width, width), width)
        both = jnp.dot(k_both, own[:, cols], preferred_element_type=jnp.float32)
        host_out[:, cols] = both[:rows]
        host_row[pl.ds(c, 1), :] = both[rows : rows + 1]

    host_row_copy = small_copy(host_row, host_row_in, 1, (diag_d, h))
    host_row_copy.start()

    spill_copy.wait()
    totals[...] = partial[:, :racks] + spill[...]
    slots = lax.broadcasted_iota(jnp.int32, (8 * shards, 128), 0)
    slot_pod = jnp.where(slots % 8 < POD_DEV, slots // 8 * POD_DEV + slots % 8, -1)
    pod_member = jnp.concatenate(
        [
            (slot_pod == pod_ref[pl.ds(k, 1), :]).astype(jnp.float32)
            for k in range(racks // 128)
        ],
        axis=1,
    )
    pod_terms[...] = lax.dot_general(
        pod_member, totals[...], NT, preferred_element_type=jnp.float32, precision=EXACT
    )

    def pod_copy(k):
        peer = lax.rem(h + k, shards)
        return pltpu.make_async_remote_copy(
            src_ref=pod_terms.at[pl.ds(pl.multiple_of(peer * 8, 8), 8), :],
            dst_ref=pod_in.at[k],
            send_sem=pod_send.at[k],
            recv_sem=pod_recv.at[k],
            device_id=(d, peer),
            device_id_type=MESH,
        )

    @pl.loop(1, shards)
    def _(k):
        pod_copy(k).start()

    rack_row[...] = jnp.dot(
        k_diag, totals[...], preferred_element_type=jnp.float32, precision=EXACT
    )
    copies = [
        small_copy(totals, far_totals, 2, (far_d, h)),
        small_copy(rack_row, rack_row_in, 3, (diag_d, h)),
        small_copy(totals, near_totals, 4, (near_d, h)),
    ]
    for copy in copies:
        copy.start()
    next_far(AHEAD + 1)

    near_copy.wait()
    k_near_half = k_near.astype(jnp.bfloat16)

    @pl.loop(0, PARTS)
    def _(c):
        cols = pl.ds(pl.multiple_of(c * width, width), width)
        host_out[:, cols] += jnp.dot(
            k_near_half, near[:, cols], preferred_element_type=jnp.float32
        )

    next_far(AHEAD + 2)
    pod_sum[...] = pod_terms[pl.ds(pl.multiple_of(h * 8, 8), 8), :]

    @pl.loop(1, shards)
    def _(k):
        pod_copy(k).wait()
        pod_sum[...] += pod_in[k]

    pod_copies = [
        small_copy(pod_sum, slab_pods.at[0], 5, (far_d, h)),
        small_copy(pod_sum, slab_pods.at[1], 6, (diag_d, h)),
        small_copy(pod_sum, slab_pods.at[2], 7, (near_d, h)),
    ]
    for copy in pod_copies:
        copy.start()

    host_row_copy.wait()
    k_far_half = k_far.astype(jnp.bfloat16)
    host_scale = 1.0 / (window * math.sqrt(day))

    def finish(c):
        cols = pl.ds(pl.multiple_of(c * width, width), width)
        far_copy(c).wait_recv()
        host_out[:, cols] = (
            host_out[:, cols]
            + jnp.dot(k_far_half, far[:, cols], preferred_element_type=jnp.float32)
            + host_row_in[pl.ds(c, 1), :]
        ) * host_scale

    @pl.loop(0, PARTS - 2)
    def _(c):
        finish(c)

    for copy in copies + pod_copies:
        copy.wait()

    def exact(a, b):
        return jnp.dot(a, b, preferred_element_type=jnp.float32, precision=EXACT)

    def exact_nt(a, b):
        return lax.dot_general(a, b, NT, preferred_element_type=jnp.float32, precision=EXACT)

    rack_scale = 1.0 / (window * math.sqrt(day * hosts / racks))
    rack_out[...] = (
        exact(k_own, totals[...])
        + exact(k_near, near_totals[...])
        + exact(k_far, far_totals[...])
        + rack_row_in[0:1, :]
    ) * rack_scale
    pod_scale = 1.0 / (window * math.sqrt(day * hosts / POD_DEV))
    pods = (
        exact_nt(pod_sum[...], k_own)
        + exact_nt(slab_pods[0], k_far)
        + exact_nt(slab_pods[1], coefficients(d, diag_d, rows, rows))
        + exact_nt(slab_pods[2], k_near)
    ) * pod_scale
    pod_out[...] = pods[:POD_DEV]

    @pl.loop(PARTS - 2, PARTS)
    def _(c):
        finish(c)

    for c in range(PARTS - AHEAD, PARTS):
        far_copy(c).wait_send()


def on_device(load, host_rack, rack_pod):
    rows, hosts = load.shape
    racks = rack_pod.shape[0]
    shards = lax.axis_size("hst")
    f32 = jnp.float32
    hbm = pl.BlockSpec(memory_space=pltpu.HBM)
    vmem = pl.BlockSpec(memory_space=pltpu.VMEM)
    shapes = (
        pltpu.VMEM((rows, hosts), f32),
        pltpu.VMEM((rows, racks), f32),
        pltpu.VMEM((POD_DEV, rows), f32),
    )
    placed = functools.partial(pltpu.with_memory_space_constraint, memory_space=pltpu.HBM)
    host, rack, pod = pl.pallas_call(
        functools.partial(kernel, shards),
        out_shape=shapes,
        in_specs=[hbm, hbm, hbm],
        out_specs=(vmem, vmem, vmem),
        scratch_shapes=[
            pltpu.VMEM((rows, hosts), load.dtype),
            pltpu.VMEM((rows, hosts), load.dtype),
            pltpu.VMEM((rows, hosts), load.dtype),
            pltpu.VMEM((hosts // 128, 128), jnp.int32),
            pltpu.VMEM((racks // 128, 128), jnp.int32),
            pltpu.VMEM((hosts // 128, 128), jnp.int32),
            pltpu.VMEM((rows, 2 * racks), f32),
            pltpu.VMEM((rows, racks), f32),
            pltpu.VMEM((rows, racks), f32),
            pltpu.VMEM((rows, racks), f32),
            pltpu.VMEM((rows, racks), f32),
            pltpu.VMEM((8 * shards, rows), f32),
            pltpu.VMEM((shards, 8, rows), f32),
            pltpu.VMEM((8, rows), f32),
            pltpu.VMEM((SLABS - 1, 8, rows), f32),
            pltpu.VMEM((8, racks), f32),
            pltpu.VMEM((8, racks), f32),
            pltpu.VMEM((PARTS, hosts // PARTS), f32),
            pltpu.VMEM((PARTS, hosts // PARTS), f32),
            pltpu.SemaphoreType.DMA((3,)),
            pltpu.SemaphoreType.DMA((2,)),
            pltpu.SemaphoreType.DMA((PARTS,)),
            pltpu.SemaphoreType.DMA((PARTS,)),
            pltpu.SemaphoreType.DMA((8,)),
            pltpu.SemaphoreType.DMA((8,)),
            pltpu.SemaphoreType.DMA((shards,)),
            pltpu.SemaphoreType.DMA((shards,)),
        ],
        compiler_params=pltpu.CompilerParams(
            collective_id=0, has_side_effects=True, vmem_limit_bytes=40 * 1024 * 1024
        ),
        cost_estimate=pl.CostEstimate(
            flops=2 * rows * hosts * (3 * rows + 2 * racks),
            bytes_accessed=rows * hosts * 10,
            transcendentals=0,
        ),
    )(
        placed(load),
        placed(host_rack.reshape(hosts // 128, 128)),
        placed(rack_pod.reshape(racks // 128, 128)),
    )
    return host, rack, pod.T


def solution(mesh):
    in_specs = (P("slab", "hst"), P("hst"), P("hst"))
    out_specs = (P("slab", "hst"), P("slab", "hst"), P("slab", "hst"))
    return jax.shard_map(
        on_device, mesh=mesh, in_specs=in_specs, out_specs=out_specs, check_vma=False
    )
```

```python
import functools
import math

import jax
import jax.numpy as jnp
from jax import lax
from jax.experimental import pallas as pl
from jax.experimental.pallas import tpu as pltpu
from jax.sharding import PartitionSpec as P

SLAB_LEN = 36
POD_DEV = 2
SLABS = 4
PARTS = 8
AHEAD = 2
MESH = pl.DeviceIdType.MESH
EXACT = lax.Precision.HIGHEST
NT = (((1,), (1,)), ((), ()))


def coefficients(target, source, out_rows, rows):
    reach = 2 * SLAB_LEN
    day = SLABS * rows
    t = target * rows + lax.broadcasted_iota(jnp.int32, (out_rows, rows), 0)
    u = source * rows + lax.broadcasted_iota(jnp.int32, (out_rows, rows), 1)
    value = jnp.where(u <= t, 2 * reach + 1, 0)
    for wrap in (-day, 0, day):
        first = jnp.maximum(u + (wrap - reach), 0)
        last = jnp.minimum(u + (wrap + reach), t)
        value = value - jnp.maximum(last - first + 1, 0)
    return value.astype(jnp.float32)


def kernel(
    shards,
    load_hbm,
    rack_hbm,
    pod_hbm,
    host_out,
    rack_out,
    pod_out,
    own,
    near,
    far,
    rack_ref,
    pod_ref,
    local_rack,
    partial,
    spill,
    totals,
    near_totals,
    far_totals,
    pod_terms,
    pod_in,
    pod_sum,
    slab_pods,
    rack_row,
    rack_row_in,
    host_row,
    host_row_in,
    load_sems,
    near_sems,
    far_send,
    far_recv,
    small_send,
    small_recv,
    pod_send,
    pod_recv,
):
    rows, hosts = own.shape
    racks = totals.shape[1]
    width = hosts // PARTS
    d = lax.axis_index("slab")
    h = lax.axis_index("hst")
    odd = lax.rem(d, 2)
    near_d = d + 1 - 2 * odd
    far_d = lax.rem(d + 3 + 2 * odd, SLABS)
    diag_d = lax.rem(d + 2, SLABS)
    window = 4 * SLAB_LEN + 1
    day = SLABS * rows

    barrier = pltpu.get_barrier_semaphore()
    for peer in (near_d, far_d, diag_d):
        pl.semaphore_signal(barrier, inc=1, device_id=(peer, h), device_id_type=MESH)

    @pl.loop(1, shards)
    def _(k):
        peer = lax.rem(h + k, shards)
        pl.semaphore_signal(barrier, inc=1, device_id=(d, peer), device_id_type=MESH)

    loads = [
        pltpu.make_async_copy(rack_hbm, rack_ref, load_sems.at[0]),
        pltpu.make_async_copy(pod_hbm, pod_ref, load_sems.at[1]),
        pltpu.make_async_copy(load_hbm, own, load_sems.at[2]),
    ]
    for copy in loads:
        copy.start()
    pl.semaphore_wait(barrier, SLABS - 1 + shards - 1)

    def far_copy(c):
        cols = pl.ds(pl.multiple_of(c * width, width), width)
        return pltpu.make_async_remote_copy(
            src_ref=load_hbm.at[:, cols],
            dst_ref=far.at[:, cols],
            send_sem=far_send.at[c],
            recv_sem=far_recv.at[c],
            device_id=(far_d, h),
            device_id_type=MESH,
        )

    def small_copy(src, dst, index, device):
        return pltpu.make_async_remote_copy(
            src_ref=src,
            dst_ref=dst,
            send_sem=small_send.at[index],
            recv_sem=small_recv.at[index],
            device_id=device,
            device_id_type=MESH,
        )

    for c in range(AHEAD):
        far_copy(c).start()
    near_copy = pltpu.make_async_remote_copy(
        src_ref=load_hbm,
        dst_ref=near,
        send_sem=near_sems.at[0],
        recv_sem=near_sems.at[1],
        device_id=(near_d, h),
        device_id_type=MESH,
    )
    near_copy.start()
    for copy in loads:
        copy.wait()
    local = rack_ref[...] - h * racks
    local_rack[...] = jnp.where(local < 0, local + racks * shards, local)

    def next_far(c):
        far_copy(c - AHEAD).wait_send()
        far_copy(c).start()

    partial[...] = jnp.zeros_like(partial)
    rack_ids = lax.broadcasted_iota(jnp.int32, (2 * racks, 128), 0)

    def add_members(c):
        cols = pl.ds(pl.multiple_of(c * width, width), width)
        member = jnp.concatenate(
            [
                (rack_ids == local_rack[pl.ds(c * (width // 128) + k, 1), :])
                .astype(jnp.float32)
                .astype(jnp.bfloat16)
                for k in range(width // 128)
            ],
            axis=1,
        )
        partial[...] += lax.dot_general(
            own[:, cols], member, NT, preferred_element_type=jnp.float32
        )

    pl.loop(0, PARTS // 2)(add_members)
    next_far(2)
    pl.loop(PARTS // 2, PARTS)(add_members)

    spill_copy = small_copy(
        partial.at[:, pl.ds(racks, racks)], spill, 0, (d, lax.rem(h + 1, shards))
    )
    spill_copy.start()
    next_far(3)

    k_own = coefficients(d, d, rows, rows)
    k_near = coefficients(d, near_d, rows, rows)
    k_far = coefficients(d, far_d, rows, rows)
    k_diag = coefficients(diag_d, d, 8, rows)
    k_both = jnp.concatenate([k_own, k_diag], 0).astype(jnp.bfloat16)

    @pl.loop(0, PARTS)
    def _(c):
        cols = pl.ds(pl.multiple_of(c * width, width), width)
        both = jnp.dot(k_both, own[:, cols], preferred_element_type=jnp.float32)
        host_out[:, cols] = both[:rows]
        host_row[pl.ds(c, 1), :] = both[rows : rows + 1]

    host_row_copy = small_copy(host_row, host_row_in, 1, (diag_d, h))
    host_row_copy.start()

    spill_copy.wait()
    totals[...] = partial[:, :racks] + spill[...]
    slots = lax.broadcasted_iota(jnp.int32, (8 * shards, 128), 0)
    slot_pod = jnp.where(slots % 8 < POD_DEV, slots // 8 * POD_DEV + slots % 8, -1)
    pod_member = jnp.concatenate(
        [
            (slot_pod == pod_ref[pl.ds(k, 1), :]).astype(jnp.float32)
            for k in range(racks // 128)
        ],
        axis=1,
    )
    pod_terms[...] = lax.dot_general(
        pod_member, totals[...], NT, preferred_element_type=jnp.float32, precision=EXACT
    )

    def pod_copy(k):
        peer = lax.rem(h + k, shards)
        return pltpu.make_async_remote_copy(
            src_ref=pod_terms.at[pl.ds(pl.multiple_of(peer * 8, 8), 8), :],
            dst_ref=pod_in.at[k],
            send_sem=pod_send.at[k],
            recv_sem=pod_recv.at[k],
            device_id=(d, peer),
            device_id_type=MESH,
        )

    @pl.loop(1, shards)
    def _(k):
        pod_copy(k).start()

    rack_row[...] = jnp.dot(
        k_diag, totals[...], preferred_element_type=jnp.float32, precision=EXACT
    )
    copies = [
        small_copy(totals, far_totals, 2, (far_d, h)),
        small_copy(rack_row, rack_row_in, 3, (diag_d, h)),
        small_copy(totals, near_totals, 4, (near_d, h)),
    ]
    for copy in copies:
        copy.start()
    next_far(4)

    near_copy.wait()
    k_near_half = k_near.astype(jnp.bfloat16)

    @pl.loop(0, PARTS)
    def _(c):
        cols = pl.ds(pl.multiple_of(c * width, width), width)
        host_out[:, cols] += jnp.dot(
            k_near_half, near[:, cols], preferred_element_type=jnp.float32
        )

    pod_sum[...] = pod_terms[pl.ds(pl.multiple_of(h * 8, 8), 8), :]

    @pl.loop(1, shards)
    def _(k):
        pod_copy(k).wait()
        pod_sum[...] += pod_in[k]

    pod_copies = [
        small_copy(pod_sum, slab_pods.at[0], 5, (far_d, h)),
        small_copy(pod_sum, slab_pods.at[1], 6, (diag_d, h)),
        small_copy(pod_sum, slab_pods.at[2], 7, (near_d, h)),
    ]
    for copy in pod_copies:
        copy.start()
    next_far(5)

    host_row_copy.wait()
    k_far_half = k_far.astype(jnp.bfloat16)
    host_scale = 1.0 / (window * math.sqrt(day))

    def finish(c):
        cols = pl.ds(pl.multiple_of(c * width, width), width)
        far_copy(c).wait_recv()
        host_out[:, cols] = (
            host_out[:, cols]
            + jnp.dot(k_far_half, far[:, cols], preferred_element_type=jnp.float32)
            + host_row_in[pl.ds(c, 1), :]
        ) * host_scale

    pl.loop(0, PARTS - 4)(finish)
    for c in range(PARTS - 4, PARTS - 2):
        finish(c)
        next_far(c + 2)

    for copy in copies + pod_copies:
        copy.wait()

    def exact(a, b):
        return jnp.dot(a, b, preferred_element_type=jnp.float32, precision=EXACT)

    def exact_nt(a, b):
        return lax.dot_general(a, b, NT, preferred_element_type=jnp.float32, precision=EXACT)

    rack_scale = 1.0 / (window * math.sqrt(day * hosts / racks))
    rack_out[...] = (
        exact(k_own, totals[...])
        + exact(k_near, near_totals[...])
        + exact(k_far, far_totals[...])
        + rack_row_in[0:1, :]
    ) * rack_scale
    pod_scale = 1.0 / (window * math.sqrt(day * hosts / POD_DEV))
    pods = (
        exact_nt(pod_sum[...], k_own)
        + exact_nt(slab_pods[0], k_far)
        + exact_nt(slab_pods[1], coefficients(d, diag_d, rows, rows))
        + exact_nt(slab_pods[2], k_near)
    ) * pod_scale
    pod_out[...] = pods[:POD_DEV]

    pl.loop(PARTS - 2, PARTS)(finish)
    for c in range(PARTS - AHEAD, PARTS):
        far_copy(c).wait_send()


def on_device(load, host_rack, rack_pod):
    rows, hosts = load.shape
    racks = rack_pod.shape[0]
    shards = lax.axis_size("hst")
    f32 = jnp.float32
    hbm = pl.BlockSpec(memory_space=pltpu.HBM)
    vmem = pl.BlockSpec(memory_space=pltpu.VMEM)
    shapes = (
        pltpu.VMEM((rows, hosts), f32),
        pltpu.VMEM((rows, racks), f32),
        pltpu.VMEM((POD_DEV, rows), f32),
    )
    placed = functools.partial(pltpu.with_memory_space_constraint, memory_space=pltpu.HBM)
    host, rack, pod = pl.pallas_call(
        functools.partial(kernel, shards),
        out_shape=shapes,
        in_specs=[hbm, hbm, hbm],
        out_specs=(vmem, vmem, vmem),
        scratch_shapes=[
            pltpu.VMEM((rows, hosts), load.dtype),
            pltpu.VMEM((rows, hosts), load.dtype),
            pltpu.VMEM((rows, hosts), load.dtype),
            pltpu.VMEM((hosts // 128, 128), jnp.int32),
            pltpu.VMEM((racks // 128, 128), jnp.int32),
            pltpu.VMEM((hosts // 128, 128), jnp.int32),
            pltpu.VMEM((rows, 2 * racks), f32),
            pltpu.VMEM((rows, racks), f32),
            pltpu.VMEM((rows, racks), f32),
            pltpu.VMEM((rows, racks), f32),
            pltpu.VMEM((rows, racks), f32),
            pltpu.VMEM((8 * shards, rows), f32),
            pltpu.VMEM((shards, 8, rows), f32),
            pltpu.VMEM((8, rows), f32),
            pltpu.VMEM((SLABS - 1, 8, rows), f32),
            pltpu.VMEM((8, racks), f32),
            pltpu.VMEM((8, racks), f32),
            pltpu.VMEM((PARTS, hosts // PARTS), f32),
            pltpu.VMEM((PARTS, hosts // PARTS), f32),
            pltpu.SemaphoreType.DMA((3,)),
            pltpu.SemaphoreType.DMA((2,)),
            pltpu.SemaphoreType.DMA((PARTS,)),
            pltpu.SemaphoreType.DMA((PARTS,)),
            pltpu.SemaphoreType.DMA((8,)),
            pltpu.SemaphoreType.DMA((8,)),
            pltpu.SemaphoreType.DMA((shards,)),
            pltpu.SemaphoreType.DMA((shards,)),
        ],
        compiler_params=pltpu.CompilerParams(
            collective_id=0, has_side_effects=True, vmem_limit_bytes=40 * 1024 * 1024
        ),
        cost_estimate=pl.CostEstimate(
            flops=2 * rows * hosts * (3 * rows + 2 * racks),
            bytes_accessed=rows * hosts * 10,
            transcendentals=0,
        ),
    )(
        placed(load),
        placed(host_rack.reshape(hosts // 128, 128)),
        placed(rack_pod.reshape(racks // 128, 128)),
    )
    return host, rack, pod.T


def solution(mesh):
    in_specs = (P("slab", "hst"), P("hst"), P("hst"))
    out_specs = (P("slab", "hst"), P("slab", "hst"), P("slab", "hst"))
    return jax.shard_map(
        on_device, mesh=mesh, in_specs=in_specs, out_specs=out_specs, check_vma=False
    )
```

```python
import functools
import math

import jax
import jax.numpy as jnp
from jax import lax
from jax.experimental import pallas as pl
from jax.experimental.pallas import tpu as pltpu
from jax.sharding import PartitionSpec as P

SLAB_LEN = 36
POD_DEV = 2
SLABS = 4
PARTS = 8
AHEAD = 3
MESH = pl.DeviceIdType.MESH
EXACT = lax.Precision.HIGHEST
NT = (((1,), (1,)), ((), ()))


def coefficients(target, source, out_rows, rows):
    reach = 2 * SLAB_LEN
    day = SLABS * rows
    t = target * rows + lax.broadcasted_iota(jnp.int32, (out_rows, rows), 0)
    u = source * rows + lax.broadcasted_iota(jnp.int32, (out_rows, rows), 1)
    value = jnp.where(u <= t, 2 * reach + 1, 0)
    for wrap in (-day, 0, day):
        first = jnp.maximum(u + (wrap - reach), 0)
        last = jnp.minimum(u + (wrap + reach), t)
        value = value - jnp.maximum(last - first + 1, 0)
    return value.astype(jnp.float32)


def kernel(
    shards,
    load_hbm,
    rack_hbm,
    pod_hbm,
    host_out,
    rack_out,
    pod_out,
    own,
    near,
    far,
    rack_ref,
    pod_ref,
    local_rack,
    partial,
    spill,
    totals,
    near_totals,
    far_totals,
    pod_terms,
    pod_in,
    pod_sum,
    slab_pods,
    rack_row,
    rack_row_in,
    host_row,
    host_row_in,
    load_sems,
    near_sems,
    far_send,
    far_recv,
    small_send,
    small_recv,
    pod_send,
    pod_recv,
):
    rows, hosts = own.shape
    racks = totals.shape[1]
    width = hosts // PARTS
    d = lax.axis_index("slab")
    h = lax.axis_index("hst")
    odd = lax.rem(d, 2)
    near_d = d + 1 - 2 * odd
    far_d = lax.rem(d + 3 + 2 * odd, SLABS)
    diag_d = lax.rem(d + 2, SLABS)
    window = 4 * SLAB_LEN + 1
    day = SLABS * rows

    barrier = pltpu.get_barrier_semaphore()
    for peer in (near_d, far_d, diag_d):
        pl.semaphore_signal(barrier, inc=1, device_id=(peer, h), device_id_type=MESH)

    @pl.loop(1, shards)
    def _(k):
        peer = lax.rem(h + k, shards)
        pl.semaphore_signal(barrier, inc=1, device_id=(d, peer), device_id_type=MESH)

    loads = [
        pltpu.make_async_copy(rack_hbm, rack_ref, load_sems.at[0]),
        pltpu.make_async_copy(pod_hbm, pod_ref, load_sems.at[1]),
        pltpu.make_async_copy(load_hbm, own, load_sems.at[2]),
    ]
    for copy in loads:
        copy.start()
    pl.semaphore_wait(barrier, SLABS - 1 + shards - 1)

    def far_copy(c):
        cols = pl.ds(pl.multiple_of(c * width, width), width)
        return pltpu.make_async_remote_copy(
            src_ref=load_hbm.at[:, cols],
            dst_ref=far.at[:, cols],
            send_sem=far_send.at[c],
            recv_sem=far_recv.at[c],
            device_id=(far_d, h),
            device_id_type=MESH,
        )

    def small_copy(src, dst, index, device):
        return pltpu.make_async_remote_copy(
            src_ref=src,
            dst_ref=dst,
            send_sem=small_send.at[index],
            recv_sem=small_recv.at[index],
            device_id=device,
            device_id_type=MESH,
        )

    for c in range(AHEAD):
        far_copy(c).start()
    near_copy = pltpu.make_async_remote_copy(
        src_ref=load_hbm,
        dst_ref=near,
        send_sem=near_sems.at[0],
        recv_sem=near_sems.at[1],
        device_id=(near_d, h),
        device_id_type=MESH,
    )
    near_copy.start()
    for copy in loads:
        copy.wait()
    local = rack_ref[...] - h * racks
    local_rack[...] = jnp.where(local < 0, local + racks * shards, local)

    def next_far(c):
        far_copy(c - AHEAD).wait_send()
        far_copy(c).start()

    partial[...] = jnp.zeros_like(partial)
    rack_ids = lax.broadcasted_iota(jnp.int32, (2 * racks, 128), 0)

    @pl.loop(0, PARTS)
    def _(c):
        cols = pl.ds(pl.multiple_of(c * width, width), width)
        member = jnp.concatenate(
            [
                (rack_ids == local_rack[pl.ds(c * (width // 128) + k, 1), :])
                .astype(jnp.float32)
                .astype(jnp.bfloat16)
                for k in range(width // 128)
            ],
            axis=1,
        )
        partial[...] += lax.dot_general(
            own[:, cols], member, NT, preferred_element_type=jnp.float32
        )

    spill_copy = small_copy(
        partial.at[:, pl.ds(racks, racks)], spill, 0, (d, lax.rem(h + 1, shards))
    )
    spill_copy.start()
    next_far(AHEAD)

    k_own = coefficients(d, d, rows, rows)
    k_near = coefficients(d, near_d, rows, rows)
    k_far = coefficients(d, far_d, rows, rows)
    k_diag = coefficients(diag_d, d, 8, rows)
    k_both = jnp.concatenate([k_own, k_diag], 0).astype(jnp.bfloat16)

    @pl.loop(0, PARTS)
    def _(c):
        cols = pl.ds(pl.multiple_of(c * width, width), width)
        both = jnp.dot(k_both, own[:, cols], preferred_element_type=jnp.float32)
        host_out[:, cols] = both[:rows]
        host_row[pl.ds(c, 1), :] = both[rows : rows + 1]

    host_row_copy = small_copy(host_row, host_row_in, 1, (diag_d, h))
    host_row_copy.start()

    spill_copy.wait()
    totals[...] = partial[:, :racks] + spill[...]
    slots = lax.broadcasted_iota(jnp.int32, (8 * shards, 128), 0)
    slot_pod = jnp.where(slots % 8 < POD_DEV, slots // 8 * POD_DEV + slots % 8, -1)
    pod_member = jnp.concatenate(
        [
            (slot_pod == pod_ref[pl.ds(k, 1), :]).astype(jnp.float32)
            for k in range(racks // 128)
        ],
        axis=1,
    )
    pod_terms[...] = lax.dot_general(
        pod_member, totals[...], NT, preferred_element_type=jnp.float32, precision=EXACT
    )

    def pod_copy(k):
        peer = lax.rem(h + k, shards)
        return pltpu.make_async_remote_copy(
            src_ref=pod_terms.at[pl.ds(pl.multiple_of(peer * 8, 8), 8), :],
            dst_ref=pod_in.at[k],
            send_sem=pod_send.at[k],
            recv_sem=pod_recv.at[k],
            device_id=(d, peer),
            device_id_type=MESH,
        )

    @pl.loop(1, shards)
    def _(k):
        pod_copy(k).start()

    rack_row[...] = jnp.dot(
        k_diag, totals[...], preferred_element_type=jnp.float32, precision=EXACT
    )
    copies = [
        small_copy(totals, far_totals, 2, (far_d, h)),
        small_copy(rack_row, rack_row_in, 3, (diag_d, h)),
        small_copy(totals, near_totals, 4, (near_d, h)),
    ]
    for copy in copies:
        copy.start()
    next_far(AHEAD + 1)

    near_copy.wait()
    k_near_half = k_near.astype(jnp.bfloat16)

    @pl.loop(0, PARTS)
    def _(c):
        cols = pl.ds(pl.multiple_of(c * width, width), width)
        host_out[:, cols] += jnp.dot(
            k_near_half, near[:, cols], preferred_element_type=jnp.float32
        )

    next_far(AHEAD + 2)
    pod_sum[...] = pod_terms[pl.ds(pl.multiple_of(h * 8, 8), 8), :]

    @pl.loop(1, shards)
    def _(k):
        pod_copy(k).wait()
        pod_sum[...] += pod_in[k]

    pod_copies = [
        small_copy(pod_sum, slab_pods.at[0], 5, (far_d, h)),
        small_copy(pod_sum, slab_pods.at[1], 6, (diag_d, h)),
        small_copy(pod_sum, slab_pods.at[2], 7, (near_d, h)),
    ]
    for copy in pod_copies:
        copy.start()

    host_row_copy.wait()
    k_far_half = k_far.astype(jnp.bfloat16)
    host_scale = 1.0 / (window * math.sqrt(day))

    def finish(c):
        cols = pl.ds(pl.multiple_of(c * width, width), width)
        far_copy(c).wait_recv()
        host_out[:, cols] = (
            host_out[:, cols]
            + jnp.dot(k_far_half, far[:, cols], preferred_element_type=jnp.float32)
            + host_row_in[pl.ds(c, 1), :]
        ) * host_scale

    pl.loop(0, PARTS - 4)(finish)
    for c in range(PARTS - 4, PARTS - 2):
        finish(c)
        far_copy(c).wait_send()
        far_copy(c + 2).start()

    for copy in copies + pod_copies:
        copy.wait()

    def exact(a, b):
        return jnp.dot(a, b, preferred_element_type=jnp.float32, precision=EXACT)

    def exact_nt(a, b):
        return lax.dot_general(a, b, NT, preferred_element_type=jnp.float32, precision=EXACT)

    rack_scale = 1.0 / (window * math.sqrt(day * hosts / racks))
    rack_out[...] = (
        exact(k_own, totals[...])
        + exact(k_near, near_totals[...])
        + exact(k_far, far_totals[...])
        + rack_row_in[0:1, :]
    ) * rack_scale
    pod_scale = 1.0 / (window * math.sqrt(day * hosts / POD_DEV))
    pods = (
        exact_nt(pod_sum[...], k_own)
        + exact_nt(slab_pods[0], k_far)
        + exact_nt(slab_pods[1], coefficients(d, diag_d, rows, rows))
        + exact_nt(slab_pods[2], k_near)
    ) * pod_scale
    pod_out[...] = pods[:POD_DEV]

    pl.loop(PARTS - 2, PARTS)(finish)
    for c in (AHEAD, PARTS - 2, PARTS - 1):
        far_copy(c).wait_send()


def on_device(load, host_rack, rack_pod):
    rows, hosts = load.shape
    racks = rack_pod.shape[0]
    shards = lax.axis_size("hst")
    f32 = jnp.float32
    hbm = pl.BlockSpec(memory_space=pltpu.HBM)
    vmem = pl.BlockSpec(memory_space=pltpu.VMEM)
    shapes = (
        pltpu.VMEM((rows, hosts), f32),
        pltpu.VMEM((rows, racks), f32),
        pltpu.VMEM((POD_DEV, rows), f32),
    )
    placed = functools.partial(pltpu.with_memory_space_constraint, memory_space=pltpu.HBM)
    host, rack, pod = pl.pallas_call(
        functools.partial(kernel, shards),
        out_shape=shapes,
        in_specs=[hbm, hbm, hbm],
        out_specs=(vmem, vmem, vmem),
        scratch_shapes=[
            pltpu.VMEM((rows, hosts), load.dtype),
            pltpu.VMEM((rows, hosts), load.dtype),
            pltpu.VMEM((rows, hosts), load.dtype),
            pltpu.VMEM((hosts // 128, 128), jnp.int32),
            pltpu.VMEM((racks // 128, 128), jnp.int32),
            pltpu.VMEM((hosts // 128, 128), jnp.int32),
            pltpu.VMEM((rows, 2 * racks), f32),
            pltpu.VMEM((rows, racks), f32),
            pltpu.VMEM((rows, racks), f32),
            pltpu.VMEM((rows, racks), f32),
            pltpu.VMEM((rows, racks), f32),
            pltpu.VMEM((8 * shards, rows), f32),
            pltpu.VMEM((shards, 8, rows), f32),
            pltpu.VMEM((8, rows), f32),
            pltpu.VMEM((SLABS - 1, 8, rows), f32),
            pltpu.VMEM((8, racks), f32),
            pltpu.VMEM((8, racks), f32),
            pltpu.VMEM((PARTS, hosts // PARTS), f32),
            pltpu.VMEM((PARTS, hosts // PARTS), f32),
            pltpu.SemaphoreType.DMA((3,)),
            pltpu.SemaphoreType.DMA((2,)),
            pltpu.SemaphoreType.DMA((PARTS,)),
            pltpu.SemaphoreType.DMA((PARTS,)),
            pltpu.SemaphoreType.DMA((8,)),
            pltpu.SemaphoreType.DMA((8,)),
            pltpu.SemaphoreType.DMA((shards,)),
            pltpu.SemaphoreType.DMA((shards,)),
        ],
        compiler_params=pltpu.CompilerParams(
            collective_id=0, has_side_effects=True, vmem_limit_bytes=40 * 1024 * 1024
        ),
        cost_estimate=pl.CostEstimate(
            flops=2 * rows * hosts * (3 * rows + 2 * racks),
            bytes_accessed=rows * hosts * 10,
            transcendentals=0,
        ),
    )(
        placed(load),
        placed(host_rack.reshape(hosts // 128, 128)),
        placed(rack_pod.reshape(racks // 128, 128)),
    )
    return host, rack, pod.T


def solution(mesh):
    in_specs = (P("slab", "hst"), P("hst"), P("hst"))
    out_specs = (P("slab", "hst"), P("slab", "hst"), P("slab", "hst"))
    return jax.shard_map(
        on_device, mesh=mesh, in_specs=in_specs, out_specs=out_specs, check_vma=False
    )
```
